32 devices in a mesh: sec: 4 (over y, x), tile: 8 (over z, core).
Axes of the slice: x: 2, y: 2, z: 4, core: 2. Of those that a mesh axis runs over, the one named last changes fastest.
Arguments:
- images: bfloat16 [4, 640, 760], P('sec', 'tile'), may hold values from -30 to 30
- patch_mask: int32 [4, 16, 16], P('sec', 'tile'), may hold values 0 or 1
- springs: int32 [4, 2, 16, 16], P('sec', None, 'tile'), may hold values 0 or 1
- groups: int32 [4], replicated, may hold values from 0 to 1, never falling along the last dimension, each value on 1 to 3 neighbouring positions
Outputs:
- flows: float32 [4, 2, 2, 16, 16], P('sec', None, None, 'tile')
- displacement: float32 [4, 2, 16, 16], P('sec', None, 'tile')
The draws below stay inside these ranges and needn't reach their ends.
All inputs are finite; a program needn't handle non-finite values. No bound on the sum of `patch_mask` or of `springs` on one device may be relied on, other than what follows from the above.
Results may differ from the reference program's by a relative error of at most 0.012.
The reference program's roundings to bfloat16 on the way (of `patches`) count: a program that leaves them out, or rounds other values in their place, can miss the bound.
Values may be sent and summed in bfloat16 or wider, within the bound.
A program may use at most 448 MiB of HBM per device.

```python
import math
import jax
import jax.numpy as jnp
import numpy as np
from jax import lax

P_SIZE = 160
STRIDE = 40
NC = 16
RELAX = 4
WCOLS = 760
NODE_ROWS = 16
H = 640
NSEC = 4


def draw_images(key, part):
    key = jax.random.fold_in(key, 11)
    base_key, shift_key, noise_key = jax.random.split(key, 3)
    reach = max(STRIDE // 6, 1)
    blocks_wide = (WCOLS + STRIDE - 1) // STRIDE
    base = jax.random.normal(base_key, (H + 2 * reach, WCOLS + 2 * reach), jnp.float32)
    offsets = jax.random.randint(shift_key, (2, NSEC, NODE_ROWS, blocks_wide), -reach, reach + 1)
    row_ids = jnp.arange(H, dtype=jnp.int32)
    col_ids = jnp.arange(WCOLS, dtype=jnp.int32)
    row_block = row_ids // STRIDE
    col_block = col_ids // STRIDE
    off_rows = offsets[0][:, row_block][:, :, col_block]
    off_cols = offsets[1][:, row_block][:, :, col_block]
    source_rows = row_ids[None, :, None] + reach - off_rows
    source_cols = col_ids[None, None, :] + reach - off_cols
    texture = base[source_rows, source_cols]
    noise = jax.random.normal(noise_key, (NSEC, H, WCOLS), jnp.float32)
    value = 0.775 * texture + 0.632 * noise
    return jnp.clip(value, -30.0, 30.0).astype(jnp.bfloat16)


def plant(drawn, key, smallest, high):
    longest = drawn.shape.index(max(drawn.shape))
    spots = []
    for shift in (0, 1):
        where = [jax.random.randint(jax.random.fold_in(key, axis), (), 0, length) for axis, length in enumerate(drawn.shape)]
        where[longest] = (where[longest] + shift) % drawn.shape[longest]
        spots.append(tuple(where))
    return drawn.at[spots[0]].set(smallest).at[spots[1]].set(high)


def length_profile(number_of, total, bound, skew):
    portions = [(1 << 20) // math.isqrt(rank ** skew) + 1 for rank in range(2, number_of + 1)]
    rest, holding = total - bound - (number_of - 1), [1] * (number_of - 1)
    while rest > 0:
        free = [i for i in range(number_of - 1) if holding[i] < bound]
        mass, left = sum([portions[i] for i in free]), rest
        for i in free:
            more = min(bound - holding[i], max(1, left * portions[i] // mass), rest)
            holding[i] = holding[i] + more
            rest = rest - more
    return np.array([bound] + holding)


def ragged(key, number_of, total, most, lean):
    if number_of == 2:
        one = jax.random.randint(key, (), max(1, total - most), min(most, total - 1) + 1)
        return jnp.stack([one, total - one])
    sizes = jnp.asarray(length_profile(number_of, total, most, lean), jnp.int32)
    pairs = (number_of - 1) // 2
    giver, sink = sizes[1:1 + 2 * pairs:2], sizes[2:2 + 2 * pairs:2]
    margin = jnp.minimum(giver - 1, most - sink)
    shifted = jax.random.randint(jax.random.fold_in(key, 1), (pairs,), 0, 1 << 20) % (margin + 1)
    sizes = sizes.at[1:1 + 2 * pairs:2].set(giver - shifted).at[2:2 + 2 * pairs:2].set(sink + shifted)
    return sizes[jax.random.permutation(jax.random.fold_in(key, 2), number_of)]


def setup_inputs(seed: int = 0) -> dict:
    keys = jax.random.split(jax.random.key(seed), 5)
    images = draw_images(jax.random.fold_in(keys[4], 71), 0)
    patch_mask = plant((jax.random.randint(keys[1], (NSEC, NODE_ROWS, NC), 0, 5) < 4).astype(jnp.int32), jax.random.fold_in(keys[1], 1), 0, 1)
    springs = plant((jax.random.randint(keys[2], (NSEC, 2, NODE_ROWS, NC), 0, 10) < 9).astype(jnp.int32), jax.random.fold_in(keys[2], 1), 0, 1)
    groups = jnp.searchsorted(jnp.cumsum(ragged(keys[3], 2, NSEC, NSEC - 1, 0)), jnp.arange(NSEC), side="right").astype(jnp.int32)
    return {"images": images, "patch_mask": patch_mask, "springs": springs, "groups": groups}


spring_stiffness = 1.0
flow_pull = 0.5
step_size = 0.2
sharpness = 25.0


def transform_tables():
    indices = jnp.arange(P_SIZE, dtype=jnp.int32)
    turns = (indices[:, None] * indices[None, :]) % P_SIZE
    angle = turns.astype(jnp.float32) * (2.0 * math.pi / P_SIZE)
    return jnp.cos(angle).astype(jnp.bfloat16), jnp.sin(angle).astype(jnp.bfloat16)


def left_product(matrix, stack):
    return jnp.einsum("jk,nkl->njl", matrix.astype(jnp.float32), stack.astype(jnp.float32), precision=lax.Precision.HIGHEST)


def right_product(stack, matrix):
    return jnp.einsum("njk,kl->njl", stack.astype(jnp.float32), matrix.astype(jnp.float32), precision=lax.Precision.HIGHEST)


def forward(patches, cosine_table, sine_table):
    real_one = left_product(cosine_table, patches).astype(jnp.bfloat16)
    imag_one = (-left_product(sine_table, patches)).astype(jnp.bfloat16)
    real_two = (right_product(real_one, cosine_table) + right_product(imag_one, sine_table)).astype(jnp.bfloat16)
    imag_two = (right_product(imag_one, cosine_table) - right_product(real_one, sine_table)).astype(jnp.bfloat16)
    return real_two, imag_two


def soft_peak(own_real, own_imag, other_real, other_imag, cosine_table, sine_table):
    a_real = own_real.astype(jnp.float32)
    a_imag = own_imag.astype(jnp.float32)
    b_real = other_real.astype(jnp.float32)
    b_imag = other_imag.astype(jnp.float32)
    cross_real = (a_real * b_real + a_imag * b_imag).astype(jnp.bfloat16)
    cross_imag = (a_imag * b_real - a_real * b_imag).astype(jnp.bfloat16)
    back_real = (left_product(cosine_table, cross_real) - left_product(sine_table, cross_imag)).astype(jnp.bfloat16)
    back_imag = (left_product(cosine_table, cross_imag) + left_product(sine_table, cross_real)).astype(jnp.bfloat16)
    result = right_product(back_real, cosine_table) - right_product(back_imag, sine_table)
    scores = result * (sharpness / float(P_SIZE) ** 4)
    top = jnp.max(scores, axis=(1, 2), keepdims=True)
    weights = jnp.exp(scores - top)
    total = jnp.sum(weights, axis=(1, 2))
    indices = jnp.arange(P_SIZE, dtype=jnp.int32)
    offsets = ((indices + P_SIZE // 2) % P_SIZE - P_SIZE // 2).astype(jnp.float32)
    flow_rows = jnp.sum(weights * offsets[None, :, None], axis=(1, 2)) / total
    flow_cols = jnp.sum(weights * offsets[None, None, :], axis=(1, 2)) / total
    return flow_rows, flow_cols


def pair_weights(patch_mask, groups):
    section_ids = jnp.arange(NSEC, dtype=jnp.int32)
    masks = patch_mask.astype(jnp.float32)
    result = []
    for distance in (1, 2):
        earlier = jnp.maximum(section_ids - distance, 0)
        linked = ((groups == groups[earlier]) & (section_ids >= distance)).astype(jnp.float32)
        result.append(masks * masks[earlier] * linked[:, None, None])
    return jnp.stack(result, axis=1)


def reference(images, patch_mask, springs, groups):
    cosine_table, sine_table = transform_tables()
    padded = jnp.pad(images, ((0, 0), (P_SIZE // 2, P_SIZE // 2), (0, 0)))
    row_starts = jnp.arange(NODE_ROWS, dtype=jnp.int32) * STRIDE
    col_starts = jnp.arange(NC, dtype=jnp.int32) * STRIDE

    def cut_patches(section):
        def single(row_start, col_start):
            return lax.dynamic_slice(section, (row_start, col_start), (P_SIZE, P_SIZE))
        grid = jax.vmap(jax.vmap(single, (None, 0)), (0, None))(row_starts, col_starts)
        return grid.reshape(NODE_ROWS * NC, P_SIZE, P_SIZE)

    def spectrum(section):
        real_part, imag_part = forward(cut_patches(section), cosine_table, sine_table)
        return jnp.stack([real_part, imag_part])

    spectra = lax.map(spectrum, padded)
    weights = pair_weights(patch_mask, groups)

    def pair_flows(section):
        own = spectra[section]
        pieces = []
        for distance in (1, 2):
            other = spectra[jnp.maximum(section - distance, 0)]
            flow_rows, flow_cols = soft_peak(own[0], own[1], other[0], other[1], cosine_table, sine_table)
            pieces.append(jnp.stack([flow_rows, flow_cols]))
        return jnp.stack(pieces)

    raw = lax.map(pair_flows, jnp.arange(NSEC, dtype=jnp.int32)).reshape(NSEC, 2, 2, NODE_ROWS, NC)
    flows = raw * weights[:, :, None]

    near = weights[:, 0] + weights[:, 1]
    moved = (flows[:, 0] + flows[:, 1]) / jnp.maximum(near, 1.0)[:, None]
    row_ids = jnp.arange(NODE_ROWS, dtype=jnp.int32)
    col_ids = jnp.arange(NC, dtype=jnp.int32)
    down_edges = springs[:, 0].astype(jnp.float32) * (row_ids < NODE_ROWS - 1).astype(jnp.float32)[None, :, None]
    right_edges = springs[:, 1].astype(jnp.float32) * (col_ids < NC - 1).astype(jnp.float32)[None, None, :]
    up_edges = jnp.pad(down_edges, ((0, 0), (1, 0), (0, 0)))[:, :-1]
    left_edges = jnp.pad(right_edges, ((0, 0), (0, 0), (1, 0)))[:, :, :-1]
    for sweep in range(RELAX):
        framed = jnp.pad(moved, ((0, 0), (0, 0), (1, 1), (1, 1)))
        upward = framed[:, :, :-2, 1:-1]
        downward = framed[:, :, 2:, 1:-1]
        leftward = framed[:, :, 1:-1, :-2]
        rightward = framed[:, :, 1:-1, 2:]
        force = spring_stiffness * (down_edges[:, None] * (downward - moved) + up_edges[:, None] * (upward - moved)
                                    + right_edges[:, None] * (rightward - moved) + left_edges[:, None] * (leftward - moved))
        force = force + flow_pull * (flows[:, 0] - weights[:, 0][:, None] * moved + flows[:, 1] - weights[:, 1][:, None] * moved)
        moved = moved + step_size * force
    return flows, moved
```

```python
import functools
import math

import jax
import jax.numpy as jnp
import numpy as np
from jax import lax
from jax.experimental import pallas as pl
from jax.experimental.pallas import tpu as pltpu
from jax.sharding import PartitionSpec as P

P_SIZE = 160
STRIDE = 40
PR = 2
NC = 16
RELAX = 4
HALF = 80
ABOVE = 48
ROWS = 2 * HALF + ABOVE
FOLD = 96
WIDE = 768
SHIFT = 64
TILES = P_SIZE // 8

spring_stiffness = 1.0
flow_pull = 0.5
step_size = 0.2
sharpness = 25.0


def full_tables():
    indices = np.arange(P_SIZE)
    angle = (indices[:, None] * indices[None, :] % P_SIZE).astype(np.float32) * np.float32(
        2.0 * math.pi / P_SIZE
    )
    exact = angle.astype(np.float64)
    cosine = np.cos(exact).astype(np.float32).astype(jnp.bfloat16).astype(np.float32)
    sine = np.sin(exact).astype(np.float32).astype(jnp.bfloat16).astype(np.float32)
    return cosine, sine


def folded_tables():
    cosine, sine = full_tables()
    kept = HALF + 1
    first = np.zeros((PR, 2, FOLD, ROWS), np.float32)
    for node_row in range(PR):
        rows = slice(node_row * STRIDE, node_row * STRIDE + P_SIZE)
        first[node_row, 0, :kept, rows] = cosine[:kept]
        first[node_row, 1, :kept, rows] = sine[:kept]
    second = np.zeros((8, 256, 256), np.float32)
    for case in range(8):
        offset = STRIDE * case % SHIFT
        second[case, offset : offset + P_SIZE, :kept] = cosine[:, :kept]
        second[case, offset : offset + P_SIZE, 128 : 128 + kept] = sine[:, :kept]
    twice = np.full((kept,), 2.0, np.float32)
    twice[0] = twice[HALF] = 1.0
    third = np.zeros((P_SIZE, 2 * FOLD), np.float32)
    third[:, :kept] = cosine[:, :kept] * twice
    third[:, FOLD : FOLD + kept] = -2.0 * sine[:, :kept]
    fourth = np.zeros((256, P_SIZE), np.float32)
    fourth[:kept] = cosine[:kept] * twice[:, None]
    fourth[128 : 128 + kept] = -2.0 * sine[:kept]
    offsets = (np.arange(P_SIZE) + HALF) % P_SIZE - HALF
    sums = np.zeros((8, P_SIZE), np.float32)
    sums[0] = 1.0
    sums[1] = offsets
    made = [
        table.astype(jnp.bfloat16)
        for table in (first.reshape(PR * 2 * FOLD, ROWS), second, third, fourth)
    ]
    return made + [sums]


def dot(left, right):
    return jnp.dot(left, right, preferred_element_type=jnp.float32)


def phase_section(section, rows, first_ref, wide_ref, phase_ref):
    span = PR * 2 * FOLD
    wide_ref[:, : rows.shape[1]] = dot(first_ref[...], rows)
    whole = wide_ref[...]
    low = section * span
    phase_ref[0, low : low + span] = whole.astype(jnp.bfloat16)
    phase_ref[1, low : low + span] = pltpu.roll(whole, WIDE - SHIFT, 1).astype(jnp.bfloat16)


def column_step(c, second_ref, third_ref, fourth_ref, phase_ref, spec_ref, mix_ref, acc_ref):
    block = STRIDE * c // SHIFT
    start = pl.multiple_of(block // 2 * 128, 128)
    window = phase_ref[block % 2, :, pl.ds(start, 256)]
    spec_ref[...] = dot(window, second_ref[c % 8])
    factor = sharpness / float(P_SIZE) ** 4 * math.log2(math.e)

    def quarters(section, node_row):
        low = (section * PR + node_row) * 2 * FOLD
        return (
            spec_ref[low : low + FOLD, :128],
            spec_ref[low + FOLD : low + 2 * FOLD, 128:],
            spec_ref[low + FOLD : low + 2 * FOLD, :128],
            spec_ref[low : low + FOLD, 128:],
        )

    for node_row in range(PR):
        p, q, u, v = quarters(0, node_row)
        for distance in (1, 2):
            pair = (distance - 1) * PR + node_row
            pp, qq, uu, vv = quarters(distance, node_row)
            mix_ref[pair, :FOLD, :128] = (p * pp + q * qq + u * uu + v * vv).astype(jnp.bfloat16)
            mix_ref[pair, :FOLD, 128:] = (u * qq - v * pp + p * vv - q * uu).astype(jnp.bfloat16)
            mix_ref[pair, FOLD:, :128] = (p * uu - u * pp + v * qq - q * vv).astype(jnp.bfloat16)
            mix_ref[pair, FOLD:, 128:] = (p * qq + q * pp - u * vv - v * uu).astype(jnp.bfloat16)
    for pair in range(2 * PR):
        back = dot(third_ref[...], mix_ref[pair]).astype(jnp.bfloat16)
        raw = dot(back, fourth_ref[...])
        pieces = [raw[8 * i : 8 * i + 8] for i in range(TILES)]
        top = functools.reduce(jnp.maximum, pieces)
        total = jnp.zeros_like(top)
        lean = jnp.zeros_like(top)
        for i, piece in enumerate(pieces):
            weight = jnp.exp2((piece - top) * factor)
            total = total + weight
            base = float(8 * i if 8 * i < HALF else 8 * i - P_SIZE)
            if base:
                lean = lean + base * weight
        acc_ref[0, pair, c] = top
        acc_ref[1, pair, c] = total
        acc_ref[2, pair, c] = lean


def finish_pair(pair, acc_ref, sums_ref):
    factor = sharpness / float(P_SIZE) ** 4 * math.log2(math.e)
    tops = acc_ref[0, pair]
    top = jnp.max(jnp.max(tops, axis=2, keepdims=True), axis=1, keepdims=True)
    scale = jnp.exp2((tops - top) * factor)
    total = acc_ref[1, pair] * scale
    within = lax.broadcasted_iota(jnp.int32, total.shape, 1).astype(jnp.float32)
    lean = acc_ref[2, pair] * scale + within * total
    total = jnp.sum(total, axis=1)
    lean = jnp.sum(lean, axis=1)

    def over_lanes(values):
        return lax.dot_general(
            sums_ref[...],
            values,
            (((1,), (1,)), ((), ())),
            precision=lax.Precision.HIGHEST,
            preferred_element_type=jnp.float32,
        )

    sums = over_lanes(total)
    leans = over_lanes(lean)
    return leans[0:1] / sums[0:1], sums[1:2] / sums[0:1]


def flow_kernel(
    rows_ref, first_ref, second_ref, third_ref, fourth_ref, sums_ref, out_ref,
    wide_ref, phase_ref, spec_ref, mix_ref, acc_ref,
):
    wide_ref[:, WIDE - 128 :] = jnp.zeros((wide_ref.shape[0], 128), jnp.float32)
    for section in range(3):
        phase_section(section, rows_ref[section], first_ref, wide_ref, phase_ref)

    @pl.loop(0, NC)
    def _(c):
        column_step(c, second_ref, third_ref, fourth_ref, phase_ref, spec_ref, mix_ref, acc_ref)

    for pair in range(2 * PR):
        flow_rows, flow_cols = finish_pair(pair, acc_ref, sums_ref)
        distance, node_row = divmod(pair, PR)
        out_ref[distance, 0, node_row : node_row + 1] = flow_rows
        out_ref[distance, 1, node_row : node_row + 1] = flow_cols


def raw_flows(rows, interpret=False):
    return pl.pallas_call(
        flow_kernel,
        out_shape=jax.ShapeDtypeStruct((2, 2, PR, NC), jnp.float32),
        in_specs=[pl.BlockSpec(memory_space=pltpu.VMEM)] * 6,
        out_specs=pl.BlockSpec(memory_space=pltpu.VMEM),
        scratch_shapes=[
            pltpu.VMEM((PR * 2 * FOLD, WIDE), jnp.float32),
            pltpu.VMEM((2, 3 * PR * 2 * FOLD, WIDE), jnp.bfloat16),
            pltpu.VMEM((3 * PR * 2 * FOLD, 256), jnp.float32),
            pltpu.VMEM((2 * PR, 2 * FOLD, 256), jnp.bfloat16),
            pltpu.VMEM((3, 2 * PR, NC, 8, P_SIZE), jnp.float32),
        ],
        compiler_params=pltpu.CompilerParams(vmem_limit_bytes=40 * 1024 * 1024),
        cost_estimate=pl.CostEstimate(
            flops=10**10, bytes_accessed=4 * 10**6, transcendentals=1700000
        ),
        interpret=interpret,
    )(rows, *[jnp.asarray(table) for table in folded_tables()])


def from_behind(block, axis, distance):
    devices = range(lax.axis_size(axis))
    route = [(i - distance, i) for i in devices if i - distance in devices]
    return lax.ppermute(block, axis, route)


def frame_strips(stack):
    low = from_behind(stack, "tile", 1)
    high = from_behind(stack[:, :ABOVE], "tile", -1)
    return jnp.concatenate([low, stack, high], axis=1)


def per_device(images, patch_mask, springs, groups):
    strip = images[0]
    own_mask = patch_mask[0]
    strips = [strip] + [from_behind(strip, "sec", distance) for distance in (1, 2)]
    masks = [from_behind(own_mask, "sec", distance) for distance in (1, 2)]
    raw = raw_flows(frame_strips(jnp.stack(strips)))
    section = lax.axis_index("sec")
    own_float = own_mask.astype(jnp.float32)
    weights = []
    for distance in (1, 2):
        earlier = jnp.maximum(section - distance, 0)
        linked = ((groups[section] == groups[earlier]) & (section >= distance)).astype(jnp.float32)
        weights.append(own_float * masks[distance - 1].astype(jnp.float32) * linked)
    weights = jnp.stack(weights)
    flows = raw * weights[:, None]
    global_rows = PR * lax.axis_index("tile") + jnp.arange(PR, dtype=jnp.int32)
    last_row = PR * lax.axis_size("tile") - 1
    col_ids = jnp.arange(NC, dtype=jnp.int32)
    down = springs[0, 0].astype(jnp.float32) * (global_rows < last_row).astype(jnp.float32)[:, None]
    right = springs[0, 1].astype(jnp.float32) * (col_ids < NC - 1).astype(jnp.float32)[None, :]
    payload = jnp.concatenate([flows.reshape(4, PR, NC), weights, down[None], right[None]])
    reach = RELAX // PR
    around = jnp.concatenate(
        [
            payload if far == 0 else from_behind(payload, "tile", -far)
            for far in range(-reach, reach + 1)
        ],
        axis=1,
    )
    pull = around[0:2] + around[2:4]
    near = around[4] + around[5]
    moved = pull / jnp.maximum(near, 1.0)
    down = around[6]
    right = around[7]
    up = jnp.pad(down, ((1, 0), (0, 0)))[:-1]
    left = jnp.pad(right, ((0, 0), (1, 0)))[:, :-1]
    for sweep in range(RELAX):
        framed = jnp.pad(moved, ((0, 0), (1, 1), (1, 1)))
        force = spring_stiffness * (
            down * (framed[:, 2:, 1:-1] - moved)
            + up * (framed[:, :-2, 1:-1] - moved)
            + right * (framed[:, 1:-1, 2:] - moved)
            + left * (framed[:, 1:-1, :-2] - moved)
        )
        force = force + flow_pull * (pull - near * moved)
        moved = moved + step_size * force
    moved = moved[:, RELAX : RELAX + PR]
    return (flows[None], moved[None])


def solution(mesh):
    return jax.shard_map(
        per_device,
        mesh=mesh,
        in_specs=(
            P("sec", "tile", None),
            P("sec", "tile", None),
            P("sec", None, "tile", None),
            P(),
        ),
        out_specs=(P("sec", None, None, "tile", None), P("sec", None, "tile", None)),
        check_vma=False,
    )
```

```python
import functools
import math

import jax
import jax.numpy as jnp
import numpy as np
from jax import lax
from jax.experimental import pallas as pl
from jax.experimental.pallas import tpu as pltpu
from jax.sharding import PartitionSpec as P

P_SIZE = 160
STRIDE = 40
PR = 2
NC = 16
RELAX = 4
HALF = 80
ABOVE = 48
ROWS = 2 * HALF + ABOVE
FOLD = 96
WIDE = 768
SHIFT = 64
TILES = P_SIZE // 8
SLOTS = 2 * RELAX // PR + 1
KINDS = 5

spring_stiffness = 1.0
flow_pull = 0.5
step_size = 0.2
sharpness = 25.0


def full_tables():
    indices = np.arange(P_SIZE)
    angle = (indices[:, None] * indices[None, :] % P_SIZE).astype(np.float32) * np.float32(
        2.0 * math.pi / P_SIZE
    )
    exact = angle.astype(np.float64)
    cosine = np.cos(exact).astype(np.float32).astype(jnp.bfloat16).astype(np.float32)
    sine = np.sin(exact).astype(np.float32).astype(jnp.bfloat16).astype(np.float32)
    return cosine, sine


def folded_tables():
    cosine, sine = full_tables()
    kept = HALF + 1
    first = np.zeros((PR, 2, FOLD, ROWS), np.float32)
    for node_row in range(PR):
        rows = slice(node_row * STRIDE, node_row * STRIDE + P_SIZE)
        first[node_row, 0, :kept, rows] = cosine[:kept]
        first[node_row, 1, :kept, rows] = sine[:kept]
    second = np.zeros((8, 256, 256), np.float32)
    for case in range(8):
        offset = STRIDE * case % SHIFT
        second[case, offset : offset + P_SIZE, :kept] = cosine[:, :kept]
        second[case, offset : offset + P_SIZE, 128 : 128 + kept] = sine[:, :kept]
    twice = np.full((kept,), 2.0, np.float32)
    twice[0] = twice[HALF] = 1.0
    third = np.zeros((P_SIZE, 2 * FOLD), np.float32)
    third[:, :kept] = cosine[:, :kept] * twice
    third[:, FOLD : FOLD + kept] = -2.0 * sine[:, :kept]
    fourth = np.zeros((256, P_SIZE), np.float32)
    fourth[:kept] = cosine[:kept] * twice[:, None]
    fourth[128 : 128 + kept] = -2.0 * sine[:kept]
    offsets = (np.arange(P_SIZE) + HALF) % P_SIZE - HALF
    sums = np.zeros((8, P_SIZE), np.float32)
    sums[0] = 1.0
    sums[1] = offsets
    made = [
        table.astype(jnp.bfloat16)
        for table in (first.reshape(PR * 2 * FOLD, ROWS), second, third, fourth)
    ]
    return made + [sums]


def dot(left, right):
    return jnp.dot(left, right, preferred_element_type=jnp.float32)


def phase_section(section, rows, first_ref, wide_ref, phase_ref):
    wide_ref[:, : rows.shape[1]] = dot(first_ref[...], rows)
    whole = wide_ref[...]
    phase_ref[section, 0] = whole.astype(jnp.bfloat16)
    phase_ref[section, 1] = pltpu.roll(whole, WIDE - SHIFT, 1).astype(jnp.bfloat16)


def column_spectrum(c, section, phase_ref, second_ref):
    block = STRIDE * c // SHIFT
    start = pl.multiple_of(block // 2 * 128, 128)
    window = phase_ref[section, block % 2, :, pl.ds(start, 256)]
    return dot(window, second_ref[c % 8])


def quarters(ref, node_row):
    low = node_row * 2 * FOLD
    return (
        ref[low : low + FOLD, :128],
        ref[low + FOLD : low + 2 * FOLD, 128:],
        ref[low + FOLD : low + 2 * FOLD, :128],
        ref[low : low + FOLD, 128:],
    )


def column_step(c, distance, own_ref, spec_ref, mix_ref, acc_ref, third_ref, fourth_ref):
    factor = sharpness / float(P_SIZE) ** 4 * math.log2(math.e)
    for node_row in range(PR):
        p, q, u, v = quarters(own_ref.at[c], node_row)
        pp, qq, uu, vv = quarters(spec_ref, node_row)
        mix_ref[node_row, :FOLD, :128] = (p * pp + q * qq + u * uu + v * vv).astype(jnp.bfloat16)
        mix_ref[node_row, :FOLD, 128:] = (u * qq - v * pp + p * vv - q * uu).astype(jnp.bfloat16)
        mix_ref[node_row, FOLD:, :128] = (p * uu - u * pp + v * qq - q * vv).astype(jnp.bfloat16)
        mix_ref[node_row, FOLD:, 128:] = (p * qq + q * pp - u * vv - v * uu).astype(jnp.bfloat16)
    for node_row in range(PR):
        pair = (distance - 1) * PR + node_row
        back = dot(third_ref[...], mix_ref[node_row]).astype(jnp.bfloat16)
        raw = dot(back, fourth_ref[...])
        pieces = [raw[8 * i : 8 * i + 8] for i in range(TILES)]
        top = functools.reduce(jnp.maximum, pieces)
        total = jnp.zeros_like(top)
        lean = jnp.zeros_like(top)
        for i, piece in enumerate(pieces):
            weight = jnp.exp2((piece - top) * factor)
            total = total + weight
            base = float(8 * i if 8 * i < HALF else 8 * i - P_SIZE)
            if base:
                lean = lean + base * weight
        acc_ref[0, pair, c] = top
        acc_ref[1, pair, c] = total
        acc_ref[2, pair, c] = lean


def finish_pair(pair, acc_ref, sums_ref):
    factor = sharpness / float(P_SIZE) ** 4 * math.log2(math.e)
    tops = acc_ref[0, pair]
    top = jnp.max(jnp.max(tops, axis=2, keepdims=True), axis=1, keepdims=True)
    scale = jnp.exp2((tops - top) * factor)
    total = acc_ref[1, pair] * scale
    within = lax.broadcasted_iota(jnp.int32, total.shape, 1).astype(jnp.float32)
    lean = acc_ref[2, pair] * scale + within * total
    total = jnp.sum(total, axis=1)
    lean = jnp.sum(lean, axis=1)

    def over_lanes(values):
        return lax.dot_general(
            sums_ref[...],
            values,
            (((1,), (1,)), ((), ())),
            precision=lax.Precision.HIGHEST,
            preferred_element_type=jnp.float32,
        )

    sums = over_lanes(total)
    leans = over_lanes(lean)
    return leans[0:1] / sums[0:1], sums[1:2] / sums[0:1]


def relax(pay_ref, field_ref, out_ref):
    field_ref[...] = jnp.zeros_like(field_ref)
    for slot in range(SLOTS):
        for kind in range(KINDS):
            field_ref[kind, PR * slot : PR * slot + PR] = pay_ref[
                slot, PR * kind : PR * kind + PR
            ]
    near = field_ref[2]
    down = field_ref[3]
    right = field_ref[4]
    rows = down.shape[0]
    up = pltpu.roll(down, 1, 0)
    left = pltpu.roll(right, 1, 1)
    for part in range(2):
        pull = field_ref[part]
        moved = pull / jnp.maximum(near, 1.0)
        for sweep in range(RELAX):
            force = spring_stiffness * (
                down * (pltpu.roll(moved, rows - 1, 0) - moved)
                + up * (pltpu.roll(moved, 1, 0) - moved)
                + right * (pltpu.roll(moved, 127, 1) - moved)
                + left * (pltpu.roll(moved, 1, 1) - moved)
            )
            force = force + flow_pull * (pull - near * moved)
            moved = moved + step_size * force
        out_ref[part] = moved[RELAX : RELAX + PR, :NC]


def mesh_kernel(
    sections, tiles,
    groups_ref, strip_ref, mask_ref, springs_ref, first_ref, third_ref, fourth_ref, sums_ref,
    second_hbm,
    flows_ref, moved_ref,
    rows_ref, masks_ref, pay_ref, second_ref, wide_ref, phase_ref, own_ref, spec_ref, mix_ref,
    acc_ref, field_ref, send_sem, recv_sem, table_sem,
):
    sec = lax.axis_index("sec")
    tile = lax.axis_index("tile")
    fill = pltpu.make_async_copy(second_hbm, second_ref, table_sem)
    fill.start()

    pay_ref[...] = jnp.zeros_like(pay_ref)
    barrier = pltpu.get_barrier_semaphore()
    expected = 0
    for axis, here, size in (("sec", sec, sections), ("tile", tile, tiles)):
        for far in (-2, -1, 1, 2):
            there = here + far
            present = (there >= 0) & (there < size)

            @pl.when(present)
            def _():
                pl.semaphore_signal(
                    barrier, inc=1, device_id={axis: there}, device_id_type=pl.DeviceIdType.MESH
                )

            expected = expected + present.astype(jnp.int32)

    for distance in (1, 2):

        @pl.when(sec < distance)
        def _():
            rows_ref[distance] = jnp.zeros(rows_ref.shape[1:], rows_ref.dtype)
            masks_ref[distance - 1] = jnp.zeros(masks_ref.shape[1:], masks_ref.dtype)

    @pl.when(tile == 0)
    def _():
        rows_ref[:, :HALF] = jnp.zeros((3, HALF, rows_ref.shape[2]), rows_ref.dtype)

    @pl.when(tile == tiles - 1)
    def _():
        rows_ref[:, 2 * HALF :] = jnp.zeros((3, ABOVE, rows_ref.shape[2]), rows_ref.dtype)

    wide_ref[:, WIDE - 128 :] = jnp.zeros((wide_ref.shape[0], 128), jnp.float32)
    pl.semaphore_wait(barrier, expected)

    class Hop:
        def __init__(self, number, source, target, axis, far, held=None):
            here, size = (sec, sections) if axis == "sec" else (tile, tiles)
            self.sends = (here + far >= 0) & (here + far < size)
            self.gets = (here - far >= 0) & (here - far < size)
            if held is not None:
                self.sends = self.sends & held
                self.gets = self.gets & held
            self.copy = pltpu.make_async_remote_copy(
                src_ref=source,
                dst_ref=target,
                send_sem=send_sem.at[number],
                recv_sem=recv_sem.at[number],
                device_id={axis: here + far},
                device_id_type=pl.DeviceIdType.MESH,
            )

        def start(self):
            pl.when(self.sends)(self.copy.start)

        def arrive(self):
            pl.when(self.gets)(self.copy.wait_recv)

        def finish(self):
            pl.when(self.sends)(self.copy.wait_send)

    across = [
        Hop(k, strip_ref, rows_ref.at[k + 1, pl.ds(HALF, HALF)], "sec", k + 1) for k in range(2)
    ]
    marks = [Hop(2 + k, mask_ref, masks_ref.at[k], "sec", k + 1) for k in range(2)]
    beside = []
    for k in range(3):
        held = None if k == 0 else sec >= k
        whole = strip_ref if k == 0 else rows_ref.at[k, pl.ds(HALF, HALF)]
        edge = strip_ref.at[pl.ds(0, ABOVE)] if k == 0 else rows_ref.at[k, pl.ds(HALF, ABOVE)]
        beside.append(
            [
                Hop(4 + 2 * k, whole, rows_ref.at[k, pl.ds(0, HALF)], "tile", 1, held),
                Hop(5 + 2 * k, edge, rows_ref.at[k, pl.ds(2 * HALF, ABOVE)], "tile", -1, held),
            ]
        )
    middle = SLOTS // 2
    spread = [
        Hop(10 + i, pay_ref.at[middle], pay_ref.at[middle - far], "tile", far)
        for i, far in enumerate((-1, 1, -2, 2))
    ]
    for hop in across + beside[0] + marks:
        hop.start()
    rows_ref[0, HALF : 2 * HALF] = strip_ref[...]
    across[0].arrive()
    for hop in beside[1]:
        hop.start()
    for hop in beside[0]:
        hop.arrive()
    phase_section(0, rows_ref[0], first_ref, wide_ref, phase_ref)
    fill.wait()
    across[1].arrive()
    for hop in beside[2]:
        hop.start()

    @pl.loop(0, NC)
    def _(c):
        own_ref[c] = column_spectrum(c, 0, phase_ref, second_ref)

    for distance in (1, 2):
        for hop in beside[distance]:
            hop.arrive()
        phase_section(distance, rows_ref[distance], first_ref, wide_ref, phase_ref)

        @pl.loop(0, NC)
        def _(c):
            spec_ref[...] = column_spectrum(c, distance, phase_ref, second_ref)
            column_step(
                c, distance, own_ref, spec_ref, mix_ref, acc_ref, third_ref, fourth_ref
            )

    for hop in marks:
        hop.arrive()
    own_mask = mask_ref[...].astype(jnp.float32)
    pulls = [[0.0, 0.0], [0.0, 0.0]]
    near = jnp.zeros((PR, NC), jnp.float32)
    for distance in (1, 2):
        earlier = jnp.maximum(sec - distance, 0)
        linked = (groups_ref[sec] == groups_ref[earlier]) & (sec >= distance)
        weight = own_mask * masks_ref[distance - 1].astype(jnp.float32)
        weight = weight * jnp.where(linked, 1.0, 0.0)
        near = near + weight
        for node_row in range(PR):
            found = finish_pair((distance - 1) * PR + node_row, acc_ref, sums_ref)
            for part in range(2):
                flow = found[part] * weight[node_row : node_row + 1]
                flows_ref[distance - 1, part, node_row : node_row + 1] = flow
                pulls[part][node_row] = pulls[part][node_row] + flow
    for part in range(2):
        for node_row in range(PR):
            at = PR * part + node_row
            pay_ref[middle, at : at + 1, :NC] = pulls[part][node_row]
    pay_ref[middle, 2 * PR : 3 * PR, :NC] = near
    global_rows = PR * tile + lax.broadcasted_iota(jnp.int32, (PR, NC), 0)
    col_ids = lax.broadcasted_iota(jnp.int32, (PR, NC), 1)
    pay_ref[middle, 3 * PR : 4 * PR, :NC] = jnp.where(
        global_rows < PR * tiles - 1, springs_ref[0].astype(jnp.float32), 0.0
    )
    pay_ref[middle, 4 * PR : 5 * PR, :NC] = jnp.where(
        col_ids < NC - 1, springs_ref[1].astype(jnp.float32), 0.0
    )
    for hop in spread:
        hop.start()
    for hop in spread:
        hop.arrive()
    relax(pay_ref, field_ref, moved_ref)
    for hop in across + marks + beside[0] + beside[1] + beside[2] + spread:
        hop.finish()


def per_device(images, patch_mask, springs, groups):
    sections, tiles = lax.axis_size("sec"), lax.axis_size("tile")
    first, second, third, fourth, sums = [jnp.asarray(table) for table in folded_tables()]
    strip = images[0]
    span = PR * 2 * FOLD
    vmem = pl.BlockSpec(memory_space=pltpu.VMEM)
    flows, moved = pl.pallas_call(
        functools.partial(mesh_kernel, sections, tiles),
        out_shape=(
            jax.ShapeDtypeStruct((2, 2, PR, NC), jnp.float32),
            jax.ShapeDtypeStruct((2, PR, NC), jnp.float32),
        ),
        in_specs=[pl.BlockSpec(memory_space=pltpu.SMEM)]
        + [vmem] * 7
        + [pl.BlockSpec(memory_space=pl.ANY)],
        out_specs=(vmem, vmem),
        scratch_shapes=[
            pltpu.VMEM((3, ROWS, strip.shape[1]), jnp.bfloat16),
            pltpu.VMEM((2, PR, NC), jnp.int32),
            pltpu.VMEM((SLOTS, 16, 128), jnp.float32),
            pltpu.VMEM(second.shape, jnp.bfloat16),
            pltpu.VMEM((span, WIDE), jnp.float32),
            pltpu.VMEM((3, 2, span, WIDE), jnp.bfloat16),
            pltpu.VMEM((NC, span, 256), jnp.float32),
            pltpu.VMEM((span, 256), jnp.float32),
            pltpu.VMEM((PR, 2 * FOLD, 256), jnp.bfloat16),
            pltpu.VMEM((3, 2 * PR, NC, 8, P_SIZE), jnp.float32),
            pltpu.VMEM((KINDS, 16, 128), jnp.float32),
            pltpu.SemaphoreType.DMA((14,)),
            pltpu.SemaphoreType.DMA((14,)),
            pltpu.SemaphoreType.DMA,
        ],
        compiler_params=pltpu.CompilerParams(
            vmem_limit_bytes=48 * 1024 * 1024, collective_id=0, has_side_effects=True
        ),
        cost_estimate=pl.CostEstimate(
            flops=10**10, bytes_accessed=4 * 10**6, transcendentals=1700000
        ),
    )(groups, strip, patch_mask[0], springs[0], first, third, fourth, sums, second)
    return (flows[None], moved[None])


def solution(mesh):
    return jax.shard_map(
        per_device,
        mesh=mesh,
        in_specs=(
            P("sec", "tile", None),
            P("sec", "tile", None),
            P("sec", None, "tile", None),
            P(),
        ),
        out_specs=(P("sec", None, None, "tile", None), P("sec", None, "tile", None)),
        check_vma=False,
    )
```

```python
import functools
import math

import jax
import jax.numpy as jnp
import numpy as np
from jax import lax
from jax.experimental import pallas as pl
from jax.experimental.pallas import tpu as pltpu
from jax.sharding import PartitionSpec as P

P_SIZE = 160
STRIDE = 40
PR = 2
NC = 16
RELAX = 4
HALF = 80
ABOVE = 48
ROWS = 2 * HALF + ABOVE
FOLD = 96
WIDE = 768
SHIFT = 64
TILES = P_SIZE // 8
SLOTS = 2 * RELAX // PR + 1
KINDS = 5

spring_stiffness = 1.0
flow_pull = 0.5
step_size = 0.2
sharpness = 25.0


def full_tables():
    indices = np.arange(P_SIZE)
    angle = (indices[:, None] * indices[None, :] % P_SIZE).astype(np.float32) * np.float32(
        2.0 * math.pi / P_SIZE
    )
    exact = angle.astype(np.float64)
    cosine = np.cos(exact).astype(np.float32).astype(jnp.bfloat16).astype(np.float32)
    sine = np.sin(exact).astype(np.float32).astype(jnp.bfloat16).astype(np.float32)
    return cosine, sine


def folded_tables():
    cosine, sine = full_tables()
    kept = HALF + 1
    first = np.zeros((PR, 2, FOLD, ROWS), np.float32)
    for node_row in range(PR):
        rows = slice(node_row * STRIDE, node_row * STRIDE + P_SIZE)
        first[node_row, 0, :kept, rows] = cosine[:kept]
        first[node_row, 1, :kept, rows] = sine[:kept]
    second = np.zeros((8, 256, 256), np.float32)
    for case in range(8):
        offset = STRIDE * case % SHIFT
        second[case, offset : offset + P_SIZE, :kept] = cosine[:, :kept]
        second[case, offset : offset + P_SIZE, 128 : 128 + kept] = sine[:, :kept]
    twice = np.full((kept,), 2.0, np.float32)
    twice[0] = twice[HALF] = 1.0
    third = np.zeros((P_SIZE, 2 * FOLD), np.float32)
    third[:, :kept] = cosine[:, :kept] * twice
    third[:, FOLD : FOLD + kept] = -2.0 * sine[:, :kept]
    fourth = np.zeros((256, P_SIZE), np.float32)
    fourth[:kept] = cosine[:kept] * twice[:, None]
    fourth[128 : 128 + kept] = -2.0 * sine[:kept]
    offsets = (np.arange(P_SIZE) + HALF) % P_SIZE - HALF
    sums = np.zeros((8, P_SIZE), np.float32)
    sums[0] = 1.0
    sums[1] = offsets
    made = [
        table.astype(jnp.bfloat16)
        for table in (first.reshape(PR * 2 * FOLD, ROWS), second, third, fourth)
    ]
    return made + [sums]


def dot(left, right):
    return jnp.dot(left, right, preferred_element_type=jnp.float32)


def phase_section(section, rows, first_ref, wide_ref, phase_ref):
    wide_ref[:, : rows.shape[1]] = dot(first_ref[...], rows)
    whole = wide_ref[...]
    phase_ref[section, 0] = whole.astype(jnp.bfloat16)
    phase_ref[section, 1] = pltpu.roll(whole, WIDE - SHIFT, 1).astype(jnp.bfloat16)


def column_spectrum(c, section, phase_ref, second_ref, case):
    block = STRIDE * c // SHIFT
    start = pl.multiple_of(block // 2 * 128, 128)
    window = phase_ref[section, block % 2, :, pl.ds(start, 256)]
    return dot(window, second_ref[case])


def quarters(ref, node_row):
    low = node_row * 2 * FOLD
    return (
        ref[low : low + FOLD, :128],
        ref[low + FOLD : low + 2 * FOLD, 128:],
        ref[low + FOLD : low + 2 * FOLD, :128],
        ref[low : low + FOLD, 128:],
    )


def cross_step(low, own, spec, mix):
    p, q, u, v = quarters(own, low)
    pp, qq, uu, vv = quarters(spec, low)
    mix[:FOLD, :128] = (p * pp + q * qq + u * uu + v * vv).astype(jnp.bfloat16)
    mix[:FOLD, 128:] = (u * qq - v * pp + p * vv - q * uu).astype(jnp.bfloat16)
    mix[FOLD:, :128] = (p * uu - u * pp + v * qq - q * vv).astype(jnp.bfloat16)
    mix[FOLD:, 128:] = (p * qq + q * pp - u * vv - v * uu).astype(jnp.bfloat16)


def peak_step(raw, pair, c, acc_ref):
    factor = sharpness / float(P_SIZE) ** 4 * math.log2(math.e)
    pieces = [raw[8 * i : 8 * i + 8] for i in range(TILES)]
    top = functools.reduce(jnp.maximum, pieces)
    total = jnp.zeros_like(top)
    lean = jnp.zeros_like(top)
    for i, piece in enumerate(pieces):
        weight = jnp.exp2((piece - top) * factor)
        total = total + weight
        base = float(8 * i if 8 * i < HALF else 8 * i - P_SIZE)
        if base:
            lean = lean + base * weight
    acc_ref[0, pair, c] = top
    acc_ref[1, pair, c] = total
    acc_ref[2, pair, c] = lean


def column_steps(c, distance, own_ref, spec_ref, mix_ref, back_ref, acc_ref, third_ref, fourth_ref):
    both = [(half, node_row) for half in range(2) for node_row in range(PR)]
    for i, (half, node_row) in enumerate(both):
        cross_step(node_row, own_ref.at[c + 8 * half], spec_ref.at[half], mix_ref.at[i])
    for i in range(len(both)):
        back = dot(third_ref[...], mix_ref[i])
        back_ref[i * P_SIZE : (i + 1) * P_SIZE] = back.astype(jnp.bfloat16)
    raw = dot(back_ref[...], fourth_ref[...])
    for i, (half, node_row) in enumerate(both):
        pair = (distance - 1) * PR + node_row
        peak_step(raw[i * P_SIZE : (i + 1) * P_SIZE], pair, c + 8 * half, acc_ref)


def finish_pair(pair, acc_ref, sums_ref):
    factor = sharpness / float(P_SIZE) ** 4 * math.log2(math.e)
    tops = acc_ref[0, pair]
    top = jnp.max(jnp.max(tops, axis=2, keepdims=True), axis=1, keepdims=True)
    scale = jnp.exp2((tops - top) * factor)
    total = acc_ref[1, pair] * scale
    within = lax.broadcasted_iota(jnp.int32, total.shape, 1).astype(jnp.float32)
    lean = acc_ref[2, pair] * scale + within * total
    total = jnp.sum(total, axis=1)
    lean = jnp.sum(lean, axis=1)

    def over_lanes(values):
        return lax.dot_general(
            sums_ref[...],
            values,
            (((1,), (1,)), ((), ())),
            precision=lax.Precision.HIGHEST,
            preferred_element_type=jnp.float32,
        )

    sums = over_lanes(total)
    leans = over_lanes(lean)
    return leans[0:1] / sums[0:1], sums[1:2] / sums[0:1]


def relax(pay_ref, field_ref, out_ref):
    field_ref[...] = jnp.zeros_like(field_ref)
    for slot in range(SLOTS):
        for kind in range(KINDS):
            field_ref[kind, PR * slot : PR * slot + PR] = pay_ref[
                slot, PR * kind : PR * kind + PR
            ]
    near = field_ref[2]
    down = field_ref[3]
    right = field_ref[4]
    rows = down.shape[0]
    up = pltpu.roll(down, 1, 0)
    left = pltpu.roll(right, 1, 1)
    for part in range(2):
        pull = field_ref[part]
        moved = pull / jnp.maximum(near, 1.0)
        for sweep in range(RELAX):
            force = spring_stiffness * (
                down * (pltpu.roll(moved, rows - 1, 0) - moved)
                + up * (pltpu.roll(moved, 1, 0) - moved)
                + right * (pltpu.roll(moved, 127, 1) - moved)
                + left * (pltpu.roll(moved, 1, 1) - moved)
            )
            force = force + flow_pull * (pull - near * moved)
            moved = moved + step_size * force
        out_ref[part] = moved[RELAX : RELAX + PR, :NC]


def mesh_kernel(
    sections, tiles,
    groups_ref, strip_ref, mask_hbm, springs_hbm, first_hbm, second_hbm, third_hbm, fourth_hbm,
    sums_hbm,
    flows_ref, moved_ref,
    mask_ref, springs_ref, first_ref, second_ref, third_ref, fourth_ref, sums_ref,
    rows_ref, masks_ref, pay_ref, wide_ref, phase_ref, own_ref, spec_ref, mix_ref,
    back_ref, acc_ref, field_ref, send_sem, recv_sem, table_sem,
):
    sec = lax.axis_index("sec")
    tile = lax.axis_index("tile")
    fetched = (
        (strip_ref, rows_ref.at[0, pl.ds(HALF, HALF)]),
        (first_hbm, first_ref),
        (second_hbm, second_ref),
        (third_hbm, third_ref),
        (fourth_hbm, fourth_ref),
        (sums_hbm, sums_ref),
        (mask_hbm, mask_ref),
        (springs_hbm, springs_ref),
    )
    fetches = [
        pltpu.make_async_copy(source, target, table_sem.at[i])
        for i, (source, target) in enumerate(fetched)
    ]
    for fetch in fetches:
        fetch.start()

    pay_ref[...] = jnp.zeros_like(pay_ref)
    barrier = pltpu.get_barrier_semaphore()
    expected = 0
    for axis, here, size in (("sec", sec, sections), ("tile", tile, tiles)):
        for far in (-2, -1, 1, 2):
            there = here + far
            present = (there >= 0) & (there < size)

            @pl.when(present)
            def _():
                pl.semaphore_signal(
                    barrier, inc=1, device_id={axis: there}, device_id_type=pl.DeviceIdType.MESH
                )

            expected = expected + present.astype(jnp.int32)

    for distance in (1, 2):

        @pl.when(sec < distance)
        def _():
            rows_ref[distance] = jnp.zeros(rows_ref.shape[1:], rows_ref.dtype)
            masks_ref[distance - 1] = jnp.zeros(masks_ref.shape[1:], masks_ref.dtype)

    @pl.when(tile == 0)
    def _():
        rows_ref[:, :HALF] = jnp.zeros((3, HALF, rows_ref.shape[2]), rows_ref.dtype)

    @pl.when(tile == tiles - 1)
    def _():
        rows_ref[:, 2 * HALF :] = jnp.zeros((3, ABOVE, rows_ref.shape[2]), rows_ref.dtype)

    wide_ref[:, WIDE - 128 :] = jnp.zeros((wide_ref.shape[0], 128), jnp.float32)
    pl.semaphore_wait(barrier, expected)

    class Hop:
        def __init__(self, number, source, target, axis, far, held=None):
            here, size = (sec, sections) if axis == "sec" else (tile, tiles)
            self.sends = (here + far >= 0) & (here + far < size)
            self.gets = (here - far >= 0) & (here - far < size)
            if held is not None:
                self.sends = self.sends & held
                self.gets = self.gets & held
            self.copy = pltpu.make_async_remote_copy(
                src_ref=source,
                dst_ref=target,
                send_sem=send_sem.at[number],
                recv_sem=recv_sem.at[number],
                device_id={axis: here + far},
                device_id_type=pl.DeviceIdType.MESH,
            )

        def start(self):
            pl.when(self.sends)(self.copy.start)

        def arrive(self):
            pl.when(self.gets)(self.copy.wait_recv)

        def finish(self):
            pl.when(self.sends)(self.copy.wait_send)

    across = [
        Hop(k, strip_ref, rows_ref.at[k + 1, pl.ds(HALF, HALF)], "sec", k + 1) for k in range(2)
    ]
    marks = [Hop(2 + k, mask_hbm, masks_ref.at[k], "sec", k + 1) for k in range(2)]
    beside = []
    for k in range(3):
        held = None if k == 0 else sec >= k
        whole = strip_ref if k == 0 else rows_ref.at[k, pl.ds(HALF, HALF)]
        edge = strip_ref.at[pl.ds(0, ABOVE)] if k == 0 else rows_ref.at[k, pl.ds(HALF, ABOVE)]
        beside.append(
            [
                Hop(4 + 2 * k, whole, rows_ref.at[k, pl.ds(0, HALF)], "tile", 1, held),
                Hop(5 + 2 * k, edge, rows_ref.at[k, pl.ds(2 * HALF, ABOVE)], "tile", -1, held),
            ]
        )
    middle = SLOTS // 2
    spread = [
        Hop(10 + i, pay_ref.at[middle], pay_ref.at[middle - far], "tile", far)
        for i, far in enumerate((-1, 1, -2, 2))
    ]
    for hop in across + beside[0] + marks:
        hop.start()
    for fetch in fetches:
        fetch.wait()
    across[0].arrive()
    for hop in beside[1]:
        hop.start()
    for hop in beside[0]:
        hop.arrive()
    phase_section(0, rows_ref[0], first_ref, wide_ref, phase_ref)
    across[1].arrive()
    for hop in beside[2]:
        hop.start()

    @pl.loop(0, NC // 2)
    def _(c):
        for half in range(2):
            own_ref[c + 8 * half] = column_spectrum(c + 8 * half, 0, phase_ref, second_ref, c)

    for distance in (1, 2):
        for hop in beside[distance]:
            hop.arrive()
        phase_section(distance, rows_ref[distance], first_ref, wide_ref, phase_ref)

        @pl.loop(0, NC // 2)
        def _(c):
            for half in range(2):
                spec_ref[half] = column_spectrum(c + 8 * half, distance, phase_ref, second_ref, c)
            column_steps(
                c, distance, own_ref, spec_ref, mix_ref, back_ref, acc_ref, third_ref, fourth_ref
            )

    for hop in marks:
        hop.arrive()
    own_mask = mask_ref[...].astype(jnp.float32)
    pulls = [[0.0, 0.0], [0.0, 0.0]]
    near = jnp.zeros((PR, NC), jnp.float32)
    for distance in (1, 2):
        earlier = jnp.maximum(sec - distance, 0)
        linked = (groups_ref[sec] == groups_ref[earlier]) & (sec >= distance)
        weight = own_mask * masks_ref[distance - 1].astype(jnp.float32)
        weight = weight * jnp.where(linked, 1.0, 0.0)
        near = near + weight
        for node_row in range(PR):
            found = finish_pair((distance - 1) * PR + node_row, acc_ref, sums_ref)
            for part in range(2):
                flow = found[part] * weight[node_row : node_row + 1]
                flows_ref[distance - 1, part, node_row : node_row + 1] = flow
                pulls[part][node_row] = pulls[part][node_row] + flow
    for part in range(2):
        for node_row in range(PR):
            at = PR * part + node_row
            pay_ref[middle, at : at + 1, :NC] = pulls[part][node_row]
    pay_ref[middle, 2 * PR : 3 * PR, :NC] = near
    global_rows = PR * tile + lax.broadcasted_iota(jnp.int32, (PR, NC), 0)
    col_ids = lax.broadcasted_iota(jnp.int32, (PR, NC), 1)
    pay_ref[middle, 3 * PR : 4 * PR, :NC] = jnp.where(
        global_rows < PR * tiles - 1, springs_ref[0].astype(jnp.float32), 0.0
    )
    pay_ref[middle, 4 * PR : 5 * PR, :NC] = jnp.where(
        col_ids < NC - 1, springs_ref[1].astype(jnp.float32), 0.0
    )
    for hop in spread:
        hop.start()
    for hop in spread:
        hop.arrive()
    relax(pay_ref, field_ref, moved_ref)
    for hop in across + marks + beside[0] + beside[1] + beside[2] + spread:
        hop.finish()


def per_device(images, patch_mask, springs, groups):
    sections, tiles = lax.axis_size("sec"), lax.axis_size("tile")
    first, second, third, fourth, sums = [jnp.asarray(table) for table in folded_tables()]
    strip = images[0]
    span = PR * 2 * FOLD
    vmem = pl.BlockSpec(memory_space=pltpu.VMEM)
    flows, moved = pl.pallas_call(
        functools.partial(mesh_kernel, sections, tiles),
        out_shape=(
            jax.ShapeDtypeStruct((2, 2, PR, NC), jnp.float32),
            jax.ShapeDtypeStruct((2, PR, NC), jnp.float32),
        ),
        in_specs=[pl.BlockSpec(memory_space=pltpu.SMEM)]
        + [pl.BlockSpec(memory_space=pl.ANY)] * 8,
        out_specs=(vmem, vmem),
        scratch_shapes=[
            pltpu.VMEM((PR, NC), jnp.int32),
            pltpu.VMEM((2, PR, NC), jnp.int32),
            pltpu.VMEM(first.shape, jnp.bfloat16),
            pltpu.VMEM(second.shape, jnp.bfloat16),
            pltpu.VMEM(third.shape, jnp.bfloat16),
            pltpu.VMEM(fourth.shape, jnp.bfloat16),
            pltpu.VMEM(sums.shape, jnp.float32),
            pltpu.VMEM((3, ROWS, strip.shape[1]), jnp.bfloat16),
            pltpu.VMEM((2, PR, NC), jnp.int32),
            pltpu.VMEM((SLOTS, 16, 128), jnp.float32),
            pltpu.VMEM((span, WIDE), jnp.float32),
            pltpu.VMEM((3, 2, span, WIDE), jnp.bfloat16),
            pltpu.VMEM((NC, span, 256), jnp.float32),
            pltpu.VMEM((2, span, 256), jnp.float32),
            pltpu.VMEM((2 * PR, 2 * FOLD, 256), jnp.bfloat16),
            pltpu.VMEM((2 * PR * P_SIZE, 256), jnp.bfloat16),
            pltpu.VMEM((3, 2 * PR, NC, 8, P_SIZE), jnp.float32),
            pltpu.VMEM((KINDS, 16, 128), jnp.float32),
            pltpu.SemaphoreType.DMA((14,)),
            pltpu.SemaphoreType.DMA((14,)),
            pltpu.SemaphoreType.DMA((8,)),
        ],
        compiler_params=pltpu.CompilerParams(
            vmem_limit_bytes=60 * 1024 * 1024, collective_id=0, has_side_effects=True
        ),
        cost_estimate=pl.CostEstimate(
            flops=10**10, bytes_accessed=4 * 10**6, transcendentals=1700000
        ),
    )(groups, strip, patch_mask[0], springs[0], first, second, third, fourth, sums)
    return (flows[None], moved[None])


def solution(mesh):
    return jax.shard_map(
        per_device,
        mesh=mesh,
        in_specs=(
            P("sec", "tile", None),
            P("sec", "tile", None),
            P("sec", None, "tile", None),
            P(),
        ),
        out_specs=(P("sec", None, None, "tile", None), P("sec", None, "tile", None)),
        check_vma=False,
    )
```

```python
import functools
import math

import jax
import jax.numpy as jnp
import numpy as np
from jax import lax
from jax.experimental import pallas as pl
from jax.experimental.pallas import tpu as pltpu
from jax.sharding import PartitionSpec as P

P_SIZE = 160
STRIDE = 40
PR = 2
NC = 16
RELAX = 4
HALF = 80
ABOVE = 48
ROWS = 2 * HALF + ABOVE
FOLD = 96
WIDE = 768
SHIFT = 64
TILES = P_SIZE // 8
SLOTS = 2 * RELAX // PR + 1
KINDS = 5

spring_stiffness = 1.0
flow_pull = 0.5
step_size = 0.2
sharpness = 25.0


def full_tables():
    indices = np.arange(P_SIZE)
    angle = (indices[:, None] * indices[None, :] % P_SIZE).astype(np.float32) * np.float32(
        2.0 * math.pi / P_SIZE
    )
    exact = angle.astype(np.float64)
    cosine = np.cos(exact).astype(np.float32).astype(jnp.bfloat16).astype(np.float32)
    sine = np.sin(exact).astype(np.float32).astype(jnp.bfloat16).astype(np.float32)
    return cosine, sine


def folded_tables():
    cosine, sine = full_tables()
    kept = HALF + 1
    first = np.zeros((PR, 2, FOLD, ROWS), np.float32)
    for node_row in range(PR):
        rows = slice(node_row * STRIDE, node_row * STRIDE + P_SIZE)
        first[node_row, 0, :kept, rows] = cosine[:kept]
        first[node_row, 1, :kept, rows] = sine[:kept]
    second = np.zeros((8, 256, 256), np.float32)
    for case in range(8):
        offset = STRIDE * case % SHIFT
        second[case, offset : offset + P_SIZE, :kept] = cosine[:, :kept]
        second[case, offset : offset + P_SIZE, 128 : 128 + kept] = sine[:, :kept]
    twice = np.full((kept,), 2.0, np.float32)
    twice[0] = twice[HALF] = 1.0
    third = np.zeros((P_SIZE, 2 * FOLD), np.float32)
    third[:, :kept] = cosine[:, :kept] * twice
    third[:, FOLD : FOLD + kept] = -2.0 * sine[:, :kept]
    fourth = np.zeros((256, P_SIZE), np.float32)
    fourth[:kept] = cosine[:kept] * twice[:, None]
    fourth[128 : 128 + kept] = -2.0 * sine[:kept]
    offsets = (np.arange(P_SIZE) + HALF) % P_SIZE - HALF
    sums = np.zeros((8, P_SIZE), np.float32)
    sums[0] = 1.0
    sums[1] = offsets
    made = [
        table.astype(jnp.bfloat16)
        for table in (first.reshape(PR * 2 * FOLD, ROWS), second, third, fourth)
    ]
    return made + [sums]


def dot(left, right):
    return jnp.dot(left, right, preferred_element_type=jnp.float32)


def phase_section(section, rows, first_ref, wide_ref, phase_ref):
    wide_ref[:, : rows.shape[1]] = dot(first_ref[...], rows)
    whole = wide_ref[...]
    phase_ref[section, 0] = whole.astype(jnp.bfloat16)
    phase_ref[section, 1] = pltpu.roll(whole, WIDE - SHIFT, 1).astype(jnp.bfloat16)


def column_spectrum(c, section, phase_ref, second_ref, case):
    block = STRIDE * c // SHIFT
    start = pl.multiple_of(block // 2 * 128, 128)
    window = phase_ref[section, block % 2, :, pl.ds(start, 256)]
    return dot(window, second_ref[case])


def quarters(ref, node_row):
    low = node_row * 2 * FOLD
    return (
        ref[low : low + FOLD, :128],
        ref[low + FOLD : low + 2 * FOLD, 128:],
        ref[low + FOLD : low + 2 * FOLD, :128],
        ref[low : low + FOLD, 128:],
    )


def cross_step(low, own, spec, mix):
    p, q, u, v = quarters(own, low)
    pp, qq, uu, vv = quarters(spec, low)
    mix[:FOLD, :128] = (p * pp + q * qq + u * uu + v * vv).astype(jnp.bfloat16)
    mix[:FOLD, 128:] = (u * qq - v * pp + p * vv - q * uu).astype(jnp.bfloat16)
    mix[FOLD:, :128] = (p * uu - u * pp + v * qq - q * vv).astype(jnp.bfloat16)
    mix[FOLD:, 128:] = (p * qq + q * pp - u * vv - v * uu).astype(jnp.bfloat16)


def peak_step(raw, pair, c, acc_ref):
    factor = sharpness / float(P_SIZE) ** 4 * math.log2(math.e)
    pieces = [raw[8 * i : 8 * i + 8] for i in range(TILES)]
    top = functools.reduce(jnp.maximum, pieces)
    total = jnp.zeros_like(top)
    lean = jnp.zeros_like(top)
    for i, piece in enumerate(pieces):
        weight = jnp.exp2((piece - top) * factor)
        total = total + weight
        base = float(8 * i if 8 * i < HALF else 8 * i - P_SIZE)
        if base:
            lean = lean + base * weight
    acc_ref[0, pair, c] = top
    acc_ref[1, pair, c] = total
    acc_ref[2, pair, c] = lean


def cross_steps(c, own_ref, spec_ref, mix_ref):
    for i in range(2 * PR):
        half, node_row = divmod(i, PR)
        cross_step(node_row, own_ref.at[c + 8 * half], spec_ref.at[half], mix_ref.at[i])


def column_steps(mix_ref, back_ref, raw_ref, third_ref, fourth_ref):
    for i in range(2 * PR):
        back = dot(third_ref[...], mix_ref[i])
        back_ref[i * P_SIZE : (i + 1) * P_SIZE] = back.astype(jnp.bfloat16)
    raw_ref[...] = dot(back_ref[...], fourth_ref[...])


def peak_steps(c, distance, raw_ref, acc_ref):
    for i in range(2 * PR):
        half, node_row = divmod(i, PR)
        pair = (distance - 1) * PR + node_row
        peak_step(raw_ref[i * P_SIZE : (i + 1) * P_SIZE], pair, c + 8 * half, acc_ref)


def finish_pair(pair, acc_ref, sums_ref):
    factor = sharpness / float(P_SIZE) ** 4 * math.log2(math.e)
    tops = acc_ref[0, pair]
    top = jnp.max(jnp.max(tops, axis=2, keepdims=True), axis=1, keepdims=True)
    scale = jnp.exp2((tops - top) * factor)
    total = acc_ref[1, pair] * scale
    within = lax.broadcasted_iota(jnp.int32, total.shape, 1).astype(jnp.float32)
    lean = acc_ref[2, pair] * scale + within * total
    total = jnp.sum(total, axis=1)
    lean = jnp.sum(lean, axis=1)

    def over_lanes(values):
        return lax.dot_general(
            sums_ref[...],
            values,
            (((1,), (1,)), ((), ())),
            precision=lax.Precision.HIGHEST,
            preferred_element_type=jnp.float32,
        )

    sums = over_lanes(total)
    leans = over_lanes(lean)
    return leans[0:1] / sums[0:1], sums[1:2] / sums[0:1]


def relax(pay_ref, field_ref, out_ref):
    field_ref[...] = jnp.zeros_like(field_ref)
    for slot in range(SLOTS):
        for kind in range(KINDS):
            field_ref[kind, PR * slot : PR * slot + PR] = pay_ref[
                slot, PR * kind : PR * kind + PR
            ]
    near = field_ref[2]
    down = field_ref[3]
    right = field_ref[4]
    rows = down.shape[0]
    up = pltpu.roll(down, 1, 0)
    left = pltpu.roll(right, 1, 1)
    for part in range(2):
        pull = field_ref[part]
        moved = pull / jnp.maximum(near, 1.0)
        for sweep in range(RELAX):
            force = spring_stiffness * (
                down * (pltpu.roll(moved, rows - 1, 0) - moved)
                + up * (pltpu.roll(moved, 1, 0) - moved)
                + right * (pltpu.roll(moved, 127, 1) - moved)
                + left * (pltpu.roll(moved, 1, 1) - moved)
            )
            force = force + flow_pull * (pull - near * moved)
            moved = moved + step_size * force
        out_ref[part] = moved[RELAX : RELAX + PR, :NC]


def mesh_kernel(
    sections, tiles,
    groups_ref, strip_ref, mask_hbm, springs_hbm, first_hbm, second_hbm, third_hbm, fourth_hbm,
    sums_hbm,
    flows_ref, moved_ref,
    mask_ref, springs_ref, first_ref, second_ref, third_ref, fourth_ref, sums_ref,
    rows_ref, masks_ref, pay_ref, wide_ref, phase_ref, own_ref, spec_ref, mix_ref,
    back_ref, raw_ref, acc_ref, field_ref, send_sem, recv_sem, table_sem,
):
    sec = lax.axis_index("sec")
    tile = lax.axis_index("tile")
    fetched = (
        (strip_ref, rows_ref.at[0, pl.ds(HALF, HALF)]),
        (first_hbm, first_ref),
        (second_hbm, second_ref),
        (third_hbm, third_ref),
        (fourth_hbm, fourth_ref),
        (sums_hbm, sums_ref),
        (mask_hbm, mask_ref),
        (springs_hbm, springs_ref),
    )
    fetches = [
        pltpu.make_async_copy(source, target, table_sem.at[i])
        for i, (source, target) in enumerate(fetched)
    ]
    for fetch in fetches:
        fetch.start()

    pay_ref[...] = jnp.zeros_like(pay_ref)
    barrier = pltpu.get_barrier_semaphore()
    expected = 0
    for axis, here, size in (("sec", sec, sections), ("tile", tile, tiles)):
        for far in (-2, -1, 1, 2):
            there = here + far
            present = (there >= 0) & (there < size)

            @pl.when(present)
            def _():
                pl.semaphore_signal(
                    barrier, inc=1, device_id={axis: there}, device_id_type=pl.DeviceIdType.MESH
                )

            expected = expected + present.astype(jnp.int32)

    for distance in (1, 2):

        @pl.when(sec < distance)
        def _():
            rows_ref[distance] = jnp.zeros(rows_ref.shape[1:], rows_ref.dtype)
            masks_ref[distance - 1] = jnp.zeros(masks_ref.shape[1:], masks_ref.dtype)

    @pl.when(tile == 0)
    def _():
        rows_ref[:, :HALF] = jnp.zeros((3, HALF, rows_ref.shape[2]), rows_ref.dtype)

    @pl.when(tile == tiles - 1)
    def _():
        rows_ref[:, 2 * HALF :] = jnp.zeros((3, ABOVE, rows_ref.shape[2]), rows_ref.dtype)

    raw_ref[...] = jnp.zeros_like(raw_ref)
    wide_ref[:, WIDE - 128 :] = jnp.zeros((wide_ref.shape[0], 128), jnp.float32)
    pl.semaphore_wait(barrier, expected)

    class Hop:
        def __init__(self, number, source, target, axis, far, held=None):
            here, size = (sec, sections) if axis == "sec" else (tile, tiles)
            self.sends = (here + far >= 0) & (here + far < size)
            self.gets = (here - far >= 0) & (here - far < size)
            if held is not None:
                self.sends = self.sends & held
                self.gets = self.gets & held
            self.copy = pltpu.make_async_remote_copy(
                src_ref=source,
                dst_ref=target,
                send_sem=send_sem.at[number],
                recv_sem=recv_sem.at[number],
                device_id={axis: here + far},
                device_id_type=pl.DeviceIdType.MESH,
            )

        def start(self):
            pl.when(self.sends)(self.copy.start)

        def arrive(self):
            pl.when(self.gets)(self.copy.wait_recv)

        def finish(self):
            pl.when(self.sends)(self.copy.wait_send)

    across = [
        Hop(k, strip_ref, rows_ref.at[k + 1, pl.ds(HALF, HALF)], "sec", k + 1) for k in range(2)
    ]
    marks = [Hop(2 + k, mask_hbm, masks_ref.at[k], "sec", k + 1) for k in range(2)]
    beside = []
    for k in range(3):
        held = None if k == 0 else sec >= k
        whole = strip_ref if k == 0 else rows_ref.at[k, pl.ds(HALF, HALF)]
        edge = strip_ref.at[pl.ds(0, ABOVE)] if k == 0 else rows_ref.at[k, pl.ds(HALF, ABOVE)]
        beside.append(
            [
                Hop(4 + 2 * k, whole, rows_ref.at[k, pl.ds(0, HALF)], "tile", 1, held),
                Hop(5 + 2 * k, edge, rows_ref.at[k, pl.ds(2 * HALF, ABOVE)], "tile", -1, held),
            ]
        )
    middle = SLOTS // 2
    spread = [
        Hop(10 + i, pay_ref.at[middle], pay_ref.at[middle - far], "tile", far)
        for i, far in enumerate((-1, 1, -2, 2))
    ]
    for hop in across + beside[0] + marks:
        hop.start()
    for fetch in fetches:
        fetch.wait()
    across[0].arrive()
    for hop in beside[1]:
        hop.start()
    for hop in beside[0]:
        hop.arrive()
    phase_section(0, rows_ref[0], first_ref, wide_ref, phase_ref)

    @pl.loop(0, NC // 2)
    def _(c):
        for half in range(2):
            own_ref[c + 8 * half] = column_spectrum(c + 8 * half, 0, phase_ref, second_ref, c)

    across[1].arrive()
    for hop in beside[2]:
        hop.start()

    for distance in (1, 2):
        for hop in beside[distance]:
            hop.arrive()
        phase_section(distance, rows_ref[distance], first_ref, wide_ref, phase_ref)
        for half in range(2):
            spec_ref[half] = column_spectrum(8 * half, distance, phase_ref, second_ref, 0)

        @pl.loop(0, NC // 2)
        def _(c):
            cross_steps(c, own_ref, spec_ref, mix_ref)
            later = jnp.minimum(c + 1, NC // 2 - 1)
            for half in range(2):
                spec_ref[half] = column_spectrum(
                    later + 8 * half, distance, phase_ref, second_ref, later
                )
            peak_steps(jnp.maximum(c - 1, 0), distance, raw_ref, acc_ref)
            column_steps(mix_ref, back_ref, raw_ref, third_ref, fourth_ref)

        peak_steps(NC // 2 - 1, distance, raw_ref, acc_ref)

    for hop in marks:
        hop.arrive()
    own_mask = mask_ref[...].astype(jnp.float32)
    pulls = [[0.0, 0.0], [0.0, 0.0]]
    near = jnp.zeros((PR, NC), jnp.float32)
    for distance in (1, 2):
        earlier = jnp.maximum(sec - distance, 0)
        linked = (groups_ref[sec] == groups_ref[earlier]) & (sec >= distance)
        weight = own_mask * masks_ref[distance - 1].astype(jnp.float32)
        weight = weight * jnp.where(linked, 1.0, 0.0)
        near = near + weight
        for node_row in range(PR):
            found = finish_pair((distance - 1) * PR + node_row, acc_ref, sums_ref)
            for part in range(2):
                flow = found[part] * weight[node_row : node_row + 1]
                flows_ref[distance - 1, part, node_row : node_row + 1] = flow
                pulls[part][node_row] = pulls[part][node_row] + flow
    for part in range(2):
        for node_row in range(PR):
            at = PR * part + node_row
            pay_ref[middle, at : at + 1, :NC] = pulls[part][node_row]
    pay_ref[middle, 2 * PR : 3 * PR, :NC] = near
    global_rows = PR * tile + lax.broadcasted_iota(jnp.int32, (PR, NC), 0)
    col_ids = lax.broadcasted_iota(jnp.int32, (PR, NC), 1)
    pay_ref[middle, 3 * PR : 4 * PR, :NC] = jnp.where(
        global_rows < PR * tiles - 1, springs_ref[0].astype(jnp.float32), 0.0
    )
    pay_ref[middle, 4 * PR : 5 * PR, :NC] = jnp.where(
        col_ids < NC - 1, springs_ref[1].astype(jnp.float32), 0.0
    )
    for hop in spread:
        hop.start()
    for hop in spread:
        hop.arrive()
    relax(pay_ref, field_ref, moved_ref)
    for hop in across + marks + beside[0] + beside[1] + beside[2] + spread:
        hop.finish()


def per_device(images, patch_mask, springs, groups):
    sections, tiles = lax.axis_size("sec"), lax.axis_size("tile")
    first, second, third, fourth, sums = [jnp.asarray(table) for table in folded_tables()]
    strip = images[0]
    span = PR * 2 * FOLD
    vmem = pl.BlockSpec(memory_space=pltpu.VMEM)
    flows, moved = pl.pallas_call(
        functools.partial(mesh_kernel, sections, tiles),
        out_shape=(
            jax.ShapeDtypeStruct((2, 2, PR, NC), jnp.float32),
            jax.ShapeDtypeStruct((2, PR, NC), jnp.float32),
        ),
        in_specs=[pl.BlockSpec(memory_space=pltpu.SMEM)]
        + [pl.BlockSpec(memory_space=pl.ANY)] * 8,
        out_specs=(vmem, vmem),
        scratch_shapes=[
            pltpu.VMEM((PR, NC), jnp.int32),
            pltpu.VMEM((2, PR, NC), jnp.int32),
            pltpu.VMEM(first.shape, jnp.bfloat16),
            pltpu.VMEM(second.shape, jnp.bfloat16),
            pltpu.VMEM(third.shape, jnp.bfloat16),
            pltpu.VMEM(fourth.shape, jnp.bfloat16),
            pltpu.VMEM(sums.shape, jnp.float32),
            pltpu.VMEM((3, ROWS, strip.shape[1]), jnp.bfloat16),
            pltpu.VMEM((2, PR, NC), jnp.int32),
            pltpu.VMEM((SLOTS, 16, 128), jnp.float32),
            pltpu.VMEM((span, WIDE), jnp.float32),
            pltpu.VMEM((3, 2, span, WIDE), jnp.bfloat16),
            pltpu.VMEM((NC, span, 256), jnp.float32),
            pltpu.VMEM((2, span, 256), jnp.float32),
            pltpu.VMEM((2 * PR, 2 * FOLD, 256), jnp.bfloat16),
            pltpu.VMEM((2 * PR * P_SIZE, 256), jnp.bfloat16),
            pltpu.VMEM((2 * PR * P_SIZE, P_SIZE), jnp.float32),
            pltpu.VMEM((3, 2 * PR, NC, 8, P_SIZE), jnp.float32),
            pltpu.VMEM((KINDS, 16, 128), jnp.float32),
            pltpu.SemaphoreType.DMA((14,)),
            pltpu.SemaphoreType.DMA((14,)),
            pltpu.SemaphoreType.DMA((8,)),
        ],
        compiler_params=pltpu.CompilerParams(
            vmem_limit_bytes=60 * 1024 * 1024, collective_id=0, has_side_effects=True
        ),
        cost_estimate=pl.CostEstimate(
            flops=10**10, bytes_accessed=4 * 10**6, transcendentals=1700000
        ),
    )(groups, strip, patch_mask[0], springs[0], first, second, third, fourth, sums)
    return (flows[None], moved[None])


def solution(mesh):
    return jax.shard_map(
        per_device,
        mesh=mesh,
        in_specs=(
            P("sec", "tile", None),
            P("sec", "tile", None),
            P("sec", None, "tile", None),
            P(),
        ),
        out_specs=(P("sec", None, None, "tile", None), P("sec", None, "tile", None)),
        check_vma=False,
    )
```
